32 devices in a mesh: group: 2 (over x), lag: 16 (over z, y, core).
Axes of the slice: x: 2, y: 2, z: 4, core: 2. Of those that a mesh axis runs over, the one named last changes fastest.
Arguments:
- markov: bfloat16 [64, 32, 8192], P(('group', 'lag')), parts along dimension 0, may hold values from -40 to 40
- omega: int32 [512, 32], replicated, may hold values from -4 to 4
Outputs:
- basis_rows: float32 [64, 32, 8192], P(('group', 'lag')), parts along dimension 0
- coupled: float32 [64, 512], P('group'), parts along dimension 0
The draws below stay inside these ranges and needn't reach their ends.
There are 2 independent parts, one for each index of `group`. The reference program is written for one: setup_inputs(seed, part) draws one part's arguments, and reference() takes and returns one part's arrays. A program takes and returns all parts, laid end to end along the dimension named above; an argument that names none is the same for every part. Nothing has to cross between parts.
All inputs are finite; a program needn't handle non-finite values.
Results may differ from the reference program's by a relative error of at most 0.0003.
Values may be sent and summed in bfloat16 or wider, within the bound.
A program may use at most 128 MiB of HBM per device.

```python
import math
import jax
import jax.numpy as jnp
from jax import lax

IN = 32
RANK = 32
J = 16
P_SIZE = 8192
LAGS = 32
ROWS = 262144


def draw_markov(key, part):
    key = jax.random.fold_in(key, 11)
    key_base, key_rows, key_cols = jax.random.split(key, 3)
    lag_place = jnp.arange(LAGS, dtype=jnp.float32) / (LAGS - 1)
    col_scale = jnp.exp(jax.random.uniform(key_cols, (IN,), jnp.float32, jnp.log(0.5), jnp.log(2.0)))
    base = jnp.clip(jax.random.normal(key_base, (LAGS, IN, P_SIZE), jnp.float32), -5.5, 5.5)
    lag_scale = 3.0 ** (-lag_place)
    row_scale = jnp.exp(jax.random.uniform(key_rows, (P_SIZE,), jnp.float32, jnp.log(0.3), jnp.log(3.0)))
    values = base * lag_scale[:, None, None] * col_scale[None, :, None] * row_scale[None, None, :]
    return jnp.clip(values, -40.0, 40.0).astype(jnp.bfloat16)


def with_ends(entries, own_key, least, high):
    index_at = [jax.random.randint(jax.random.fold_in(own_key, axis), (), 0, length) for axis, length in enumerate(entries.shape)]
    main_axis = entries.shape.index(max(entries.shape))
    beside = index_at[:main_axis] + [(index_at[main_axis] + 1) % entries.shape[main_axis]] + index_at[main_axis + 1:]
    return entries.at[tuple(index_at)].set(least).at[tuple(beside)].set(high)


def setup_inputs(seed: int = 0, part: int = 0) -> dict:
    keys = jax.random.split(jax.random.key(seed), 3)
    own_keys = jax.random.split(jax.random.fold_in(keys[2], part), 3)
    markov = draw_markov(jax.random.fold_in(jax.random.fold_in(keys[2], part), 71), part)
    omega = with_ends(jax.random.randint(keys[1], (J * IN, RANK), -4, 5), jax.random.fold_in(keys[1], 1), -4, 4).astype(jnp.int32)
    return {"markov": markov, "omega": omega}


def test_matrix(omega):
    return (omega.astype(jnp.float32) * 0.25).astype(jnp.bfloat16)

def reference(markov, omega):
    zero_tail = jnp.zeros((J - 1, IN, P_SIZE), jnp.bfloat16)
    padded = jnp.concatenate([markov, zero_tail], axis=0)
    probes = test_matrix(omega)

    def sketch_row(position):
        window = lax.dynamic_slice_in_dim(padded, position, J, 0).reshape(J * IN, P_SIZE)
        return lax.dot_general(probes.astype(jnp.float32), window.astype(jnp.float32), (((0,), (0,)), ((), ())), preferred_element_type=jnp.float32)
    sketch = lax.map(sketch_row, jnp.arange(LAGS, dtype=jnp.int32))
    gram_matrix = jnp.einsum('krp,ksp->rs', sketch, sketch, precision=lax.Precision.HIGHEST) / ROWS
    factor = jnp.linalg.cholesky(gram_matrix)
    flattened = jnp.moveaxis(sketch, 1, 0).reshape(RANK, LAGS * P_SIZE)
    solved = jax.scipy.linalg.solve_triangular(factor, flattened, lower=True)
    basis_rows = jnp.moveaxis(solved.reshape(RANK, LAGS, P_SIZE), 0, 1)

    def add_row(running, position):
        window = lax.dynamic_slice_in_dim(padded, position, J, 0).reshape(J * IN, P_SIZE).astype(jnp.float32)
        single = lax.dynamic_index_in_dim(basis_rows, position, 0, keepdims=False)
        return (running + jnp.dot(single, window.T, precision=lax.Precision.HIGHEST), None)
    running, _ = lax.scan(add_row, jnp.zeros((RANK, J * IN), jnp.float32), jnp.arange(LAGS, dtype=jnp.int32))
    coupled = running / math.sqrt(ROWS)
    return (basis_rows, coupled)
```

```python
import functools
import math

import jax
import jax.numpy as jnp
from jax import lax
from jax.experimental import pallas as pl
from jax.experimental.pallas import tpu as pltpu
from jax.sharding import PartitionSpec as P

J = 16
TEAM = 4
CHUNKS = 4
HIGH = lax.Precision.HIGHEST
NT = (((1,), (1,)), ((), ()))


def split3(value):
    high = value.astype(jnp.bfloat16)
    rest = value - high.astype(jnp.float32)
    middle = rest.astype(jnp.bfloat16)
    low = (rest - middle.astype(jnp.float32)).astype(jnp.bfloat16)
    return high, middle, low


def inverse_factor(gram):
    size = gram.shape[0]
    rows = lax.broadcasted_iota(jnp.int32, (size, 128), 0)
    lanes = lax.broadcasted_iota(jnp.int32, (size, 128), 1)
    work = gram + jnp.where(lanes == rows + size, 1.0, 0.0)
    for step in range(size):
        pivot_row = work[step : step + 1, :]
        pivot = pivot_row[:, step : step + 1]
        scale = lax.rsqrt(pivot)
        scale = scale * (1.5 - 0.5 * pivot * scale * scale)
        unit_row = pivot_row * scale
        column = work[:, step : step + 1] * scale
        work = jnp.where(
            rows > step, work - column * unit_row, jnp.where(rows == step, unit_row, work)
        )
    return pltpu.roll(work, 128 - size, 1)[:, :size]


def kernel(count, x_ref, omega_ref, basis_ref, coupled_ref, halo, weights, sk, own, corr, gram_acc,
           msg, rbuf, kred, kfin, p1s, p1r, dns, dnr, fws, fwr, srs, srr, m1s, m1r, m2s, m2r):
    per, inputs, width = x_ref.shape
    rank = omega_ref.shape[1]
    quarter = width // TEAM
    piece = quarter // CHUNKS
    level_lags = per * TEAM
    reach = J - 1
    lags = halo.shape[1]
    levels = count // TEAM
    total_rows = count * per * width
    me = lax.axis_index("lag")
    level, place = me // TEAM, me % TEAM
    mates = [place, place + 1 - 2 * (place % 2), (place + 2) % TEAM, TEAM - 1 - place]
    below = lax.rem(me + count - TEAM, count)

    barrier = pltpu.get_barrier_semaphore()

    @pl.loop(1, count)
    def _(step):
        pl.semaphore_signal(barrier, inc=1, device_id={"lag": lax.rem(me + step, count)},
                            device_id_type=pl.DeviceIdType.MESH)

    pl.semaphore_wait(barrier, count - 1)

    def remote(src, dst, send, recv, target):
        return pltpu.make_async_remote_copy(
            src_ref=src, dst_ref=dst, send_sem=send, recv_sem=recv,
            device_id={"lag": target}, device_id_type=pl.DeviceIdType.MESH)

    def columns(who, k):
        return pl.ds(pl.multiple_of(who * quarter + k * piece, 128), piece)

    def spread(k, s):
        mate = mates[s]
        return remote(x_ref.at[:, :, columns(mate, k)], halo.at[k, pl.ds(per * place, per)],
                      p1s.at[k, s], p1r.at[k, place], level * TEAM + mate)

    def spread_in(k, s):
        mate = mates[s]
        dst = halo.at[k, pl.ds(per * mate, per)]
        return remote(dst, dst, p1s.at[k, s], p1r.at[k, mate], level * TEAM + mate)

    def down(k, s):
        mate = mates[s]
        src = x_ref.at[:, :, columns(place, k)] if s == 0 else halo.at[k, pl.ds(per * mate, per)]
        return remote(src, halo.at[k, pl.ds(level_lags + per * mate, per)],
                      dns.at[k, s], dnr.at[k, mate], below)

    def forward(k):
        return remote(halo.at[k, pl.ds(level_lags, reach - level_lags)],
                      halo.at[k, pl.ds(2 * level_lags, reach - level_lags)],
                      fws.at[k], fwr.at[k], below)

    def give_back(k, s):
        mate = mates[s]
        return remote(sk.at[k, pl.ds(per * mate, per)], own.at[place, k],
                      srs.at[k, s], srr.at[k, place], level * TEAM + mate)

    def give_back_in(k, s):
        mate = mates[s]
        return remote(own.at[mate, k], own.at[mate, k], srs.at[k, s], srr.at[k, mate],
                      level * TEAM + mate)

    for k in range(CHUNKS):
        for s in (2, 3, 1):
            spread(k, s).start()

    @pl.when(level > 0)
    def _():
        down(0, 0).start()

    for k in range(CHUNKS):
        halo[k, pl.ds(per * place, per)] = x_ref[:, :, columns(place, k)]
        halo[k, lags - 1] = jnp.zeros((inputs, piece), jnp.bfloat16)

    @pl.when(level >= levels - 2)
    def _():
        for k in range(CHUNKS):
            halo[k, 2 * level_lags : lags - 1] = jnp.zeros(
                (lags - 1 - 2 * level_lags, inputs, piece), jnp.bfloat16)

    @pl.when(level == levels - 1)
    def _():
        for k in range(CHUNKS):
            halo[k, level_lags : 2 * level_lags] = jnp.zeros(
                (level_lags, inputs, piece), jnp.bfloat16)

    def own_down(k):
        for s in range(TEAM):
            if s:
                spread_in(k, s).wait_recv()
            if s or k:
                @pl.when(level > 0)
                def _():
                    down(k, s).start()

    def pass_on(k):
        @pl.when(level < levels - 1)
        def _():
            for s in range(TEAM):
                down(k, s).wait_recv()

            @pl.when(level > 0)
            def _():
                forward(k).start()

    def compute(k):
        @pl.when(level < levels - 2)
        def _():
            forward(k).wait_recv()

        window = halo[k].reshape(lags * inputs, piece)
        sketch = jnp.dot(weights[...], window, preferred_element_type=jnp.float32)
        sk[k] = sketch.reshape(level_lags, rank, piece)
        for s in (2, 3, 1):
            give_back(k, s).start()
        own[place, k] = sk[k, pl.ds(per * place, per)]
        parts = split3(sketch)
        product = sum(
            lax.dot_general(part, window, NT, preferred_element_type=jnp.float32)
            for part in reversed(parts)
        )
        corr[...] = product if k == 0 else corr[...] + product
        wide = jnp.concatenate([sketch[i * rank : (i + 1) * rank] for i in range(level_lags)], axis=1)
        local = lax.dot_general(wide, wide, NT, precision=HIGH, preferred_element_type=jnp.float32)
        gram_acc[:, :rank] = local if k == 0 else gram_acc[:, :rank] + local

    own_down(0)
    own_down(1)
    gram_acc[...] = jnp.zeros_like(gram_acc)
    probes = omega_ref[...].astype(jnp.float32) * 0.25
    identity = jnp.where(
        lax.broadcasted_iota(jnp.int32, (rank, rank), 0)
        == lax.broadcasted_iota(jnp.int32, (rank, rank), 1), 1.0, 0.0)
    turned = lax.dot_general(identity, probes, NT, preferred_element_type=jnp.float32)
    band = jnp.concatenate(
        [turned, jnp.zeros((rank, weights.shape[1] - turned.shape[1]), jnp.float32)], axis=1)
    for i in range(level_lags):
        row = band if i == 0 else pltpu.roll(band, i * inputs, 1)
        weights[i * rank : (i + 1) * rank, :] = row.astype(jnp.bfloat16)
    pass_on(0)
    for k in range(2, CHUNKS):
        own_down(k)
        pass_on(k - 1)
        if k > 2:
            compute(k - 3)
    compute(CHUNKS - 3)
    pass_on(CHUNKS - 1)
    compute(CHUNKS - 2)
    compute(CHUNKS - 1)

    folded = corr[0:rank, : J * inputs]
    for i in range(1, level_lags):
        turned_back = pltpu.roll(corr[i * rank : (i + 1) * rank, :], lags * inputs - i * inputs, 1)
        folded = folded + turned_back[:, : J * inputs]
    packed = gram_acc[0:8, :]
    for b in range(1, rank // 8):
        packed = packed + pltpu.roll(gram_acc[8 * b : 8 * b + 8, :], b * rank, 1)
    tiles_across = J * inputs // 128
    tiles = (rank // 8) * tiles_across
    for d in range(count):
        msg[d, 0] = packed
        if d < tiles:
            a, b = divmod(d, tiles_across)
            msg[d, 1] = folded[8 * a : 8 * a + 8, 128 * b : 128 * b + 128]
        else:
            msg[d, 1] = jnp.zeros((8, 128), jnp.float32)

    def partial(step):
        other = lax.rem(me + step, count)
        return remote(msg.at[other], rbuf.at[me], m1s.at[step], m1r.at[me], other)

    def partial_in(step):
        other = lax.rem(me + step, count)
        return remote(msg.at[other], rbuf.at[other], m1s.at[step], m1r.at[other], other)

    def whole(step):
        other = lax.rem(me + step, count)
        return remote(kred, kfin.at[me], m2s.at[step], m2r.at[me], other)

    def whole_in(step):
        other = lax.rem(me + step, count)
        return remote(kred, kfin.at[other], m2s.at[step], m2r.at[other], other)

    @pl.loop(1, count)
    def _(step):
        partial(step).start()

    rbuf[me] = msg[me]

    @pl.loop(1, count)
    def _(step):
        partial_in(step).wait_recv()

    total = rbuf[0]
    for d in range(1, count):
        total = total + rbuf[d]
    kred[...] = total[1]
    kfin[me] = total[1]

    @pl.loop(1, count)
    def _(step):
        whole(step).start()

    lanes = lax.broadcasted_iota(jnp.int32, (8, 128), 1)
    blocks = []
    for b in range(rank // 8):
        block = total[0] if b == 0 else pltpu.roll(total[0], 128 - b * rank, 1)
        blocks.append(jnp.where(lanes < rank, block, 0.0))
    inverse = inverse_factor(jnp.concatenate(blocks, axis=0) * (1.0 / total_rows))

    for k in range(CHUNKS):
        for s in range(1, TEAM):
            give_back_in(k, s).wait_recv()
    for q in range(TEAM):
        for k in range(CHUNKS):
            for g in range(per):
                basis_ref[g, :, q * quarter + k * piece : q * quarter + (k + 1) * piece] = jnp.dot(
                    inverse, own[q, k, g], precision=HIGH, preferred_element_type=jnp.float32)

    @pl.loop(1, count)
    def _(step):
        whole_in(step).wait_recv()

    summed = jnp.concatenate(
        [jnp.concatenate([kfin[a * tiles_across + b] for b in range(tiles_across)], axis=1)
         for a in range(rank // 8)], axis=0)
    coupled_ref[...] = jnp.dot(
        inverse, summed, precision=HIGH, preferred_element_type=jnp.float32
    ) * (1.0 / math.sqrt(total_rows))

    for k in range(CHUNKS):
        for s in range(1, TEAM):
            spread(k, s).wait_send()
            give_back(k, s).wait_send()

    @pl.when(level > 0)
    def _():
        for k in range(CHUNKS):
            for s in range(TEAM):
                down(k, s).wait_send()

    @pl.when(jnp.logical_and(level > 0, level < levels - 1))
    def _():
        for k in range(CHUNKS):
            forward(k).wait_send()

    @pl.loop(1, count)
    def _(step):
        partial(step).wait_send()
        whole(step).wait_send()


def per_device(count, markov, omega):
    per, inputs, width = markov.shape
    rank = omega.shape[1]
    piece = width // TEAM // CHUNKS
    level_lags = per * TEAM
    lags = level_lags + J
    dma = pltpu.SemaphoreType.DMA
    vmem = pl.BlockSpec(memory_space=pltpu.VMEM)
    return pl.pallas_call(
        functools.partial(kernel, count),
        out_shape=(
            jax.ShapeDtypeStruct((per, rank, width), jnp.float32),
            jax.ShapeDtypeStruct((rank, J * inputs), jnp.float32),
        ),
        in_specs=[vmem, vmem],
        out_specs=(vmem, vmem),
        scratch_shapes=[
            pltpu.VMEM((CHUNKS, lags, inputs, piece), jnp.bfloat16),
            pltpu.VMEM((level_lags * rank, lags * inputs), jnp.bfloat16),
            pltpu.VMEM((CHUNKS, level_lags, rank, piece), jnp.float32),
            pltpu.VMEM((TEAM, CHUNKS, per, rank, piece), jnp.float32),
            pltpu.VMEM((level_lags * rank, lags * inputs), jnp.float32),
            pltpu.VMEM((rank, 128), jnp.float32),
            pltpu.VMEM((count, 2, 8, 128), jnp.float32),
            pltpu.VMEM((count, 2, 8, 128), jnp.float32),
            pltpu.VMEM((8, 128), jnp.float32),
            pltpu.VMEM((count, 8, 128), jnp.float32),
            dma((CHUNKS, TEAM)), dma((CHUNKS, TEAM)), dma((CHUNKS, TEAM)), dma((CHUNKS, TEAM)),
            dma((CHUNKS,)), dma((CHUNKS,)), dma((CHUNKS, TEAM)), dma((CHUNKS, TEAM)),
            dma((count,)), dma((count,)), dma((count,)), dma((count,)),
        ],
        compiler_params=pltpu.CompilerParams(
            collective_id=0, has_side_effects=True, vmem_limit_bytes=40 * 2**20
        ),
        cost_estimate=pl.CostEstimate(flops=6 * 10**9, bytes_accessed=8 * 2**20, transcendentals=0),
    )(markov, omega)


def solution(mesh):
    return jax.shard_map(
        functools.partial(per_device, mesh.shape["lag"]),
        mesh=mesh,
        in_specs=(P(("group", "lag"), None, None), P()),
        out_specs=(P(("group", "lag"), None, None), P("group", None)),
        check_vma=False,
    )
```

```python
import functools
import math

import jax
import jax.numpy as jnp
from jax import lax
from jax.experimental import pallas as pl
from jax.experimental.pallas import tpu as pltpu
from jax.sharding import PartitionSpec as P

J = 16
TEAM = 4
CHUNKS = 8
HIGH = lax.Precision.HIGHEST
NT = (((1,), (1,)), ((), ()))


def split3(value):
    high = value.astype(jnp.bfloat16)
    rest = value - high.astype(jnp.float32)
    middle = rest.astype(jnp.bfloat16)
    low = (rest - middle.astype(jnp.float32)).astype(jnp.bfloat16)
    return high, middle, low


def inverse_factor(gram):
    size = gram.shape[0]
    rows = lax.broadcasted_iota(jnp.int32, (size, 128), 0)
    lanes = lax.broadcasted_iota(jnp.int32, (size, 128), 1)
    work = gram + jnp.where(lanes == rows + size, 1.0, 0.0)
    for step in range(size):
        pivot_row = work[step : step + 1, :]
        pivot = pivot_row[:, step : step + 1]
        scale = lax.rsqrt(pivot)
        scale = scale * (1.5 - 0.5 * pivot * scale * scale)
        unit_row = pivot_row * scale
        column = work[:, step : step + 1] * scale
        work = jnp.where(
            rows > step, work - column * unit_row, jnp.where(rows == step, unit_row, work)
        )
    return pltpu.roll(work, 128 - size, 1)[:, :size]


def kernel(count, x_ref, omega_ref, basis_ref, coupled_ref, halo, weights, sk, own, corr, gram_acc,
           pack, gbuf, msg, rbuf, kred, kfin, xs, p1s, p1r, dns, dnr, fws, fwr, srs, srr, m0s, m0r, m1s, m1r,
           m2s, m2r):
    per, inputs, width = x_ref.shape
    rank = omega_ref.shape[0]
    quarter = width // TEAM
    piece = quarter // CHUNKS
    level_lags = per * TEAM
    reach = J - 1
    lags = halo.shape[1]
    levels = count // TEAM
    total_rows = count * per * width
    me = lax.axis_index("lag")
    level, place = me // TEAM, me % TEAM
    mates = [place, place + 1 - 2 * (place % 2), (place + 2) % TEAM, TEAM - 1 - place]
    below = lax.rem(me + count - TEAM, count)

    barrier = pltpu.get_barrier_semaphore()

    @pl.loop(1, count)
    def _(step):
        pl.semaphore_signal(barrier, inc=1, device_id={"lag": lax.rem(me + step, count)},
                            device_id_type=pl.DeviceIdType.MESH)

    pl.semaphore_wait(barrier, count - 1)

    def remote(src, dst, send, recv, target):
        return pltpu.make_async_remote_copy(
            src_ref=src, dst_ref=dst, send_sem=send, recv_sem=recv,
            device_id={"lag": target}, device_id_type=pl.DeviceIdType.MESH)

    def columns(who, k):
        return pl.ds(pl.multiple_of(who * quarter + k * piece, 128), piece)

    def spread(k, s):
        mate = mates[s]
        return remote(x_ref.at[:, :, columns(mate, k)], halo.at[k, pl.ds(per * place, per)],
                      p1s.at[k, s], p1r.at[k, place], level * TEAM + mate)

    def spread_in(k, s):
        mate = mates[s]
        dst = halo.at[k, pl.ds(per * mate, per)]
        return remote(dst, dst, p1s.at[k, s], p1r.at[k, mate], level * TEAM + mate)

    def down(k, s):
        mate = mates[s]
        src = x_ref.at[:, :, columns(place, k)] if s == 0 else halo.at[k, pl.ds(per * mate, per)]
        return remote(src, halo.at[k, pl.ds(level_lags + per * mate, per)],
                      dns.at[k, s], dnr.at[k, mate], below)

    def forward(k):
        return remote(halo.at[k, pl.ds(level_lags, reach - level_lags)],
                      halo.at[k, pl.ds(2 * level_lags, reach - level_lags)],
                      fws.at[k], fwr.at[k], below)

    def give_back(k, s):
        mate = mates[s]
        return remote(sk.at[k, pl.ds(per * mate, per)], own.at[place, k],
                      srs.at[k, s], srr.at[k, place], level * TEAM + mate)

    def give_back_in(k, s):
        mate = mates[s]
        return remote(own.at[mate, k], own.at[mate, k], srs.at[k, s], srr.at[k, mate],
                      level * TEAM + mate)

    def keep(k):
        return pltpu.make_async_copy(x_ref.at[:, :, columns(place, k)],
                                     halo.at[k, pl.ds(per * place, per)], xs.at[k])

    for k in range(CHUNKS):
        for s in (2, 3, 1):
            spread(k, s).start()

        @pl.when(level > 0)
        def _():
            down(k, 0).start()

        keep(k).start()

    for k in range(CHUNKS):
        halo[k, lags - 1] = jnp.zeros((inputs, piece), jnp.bfloat16)

    @pl.when(level >= levels - 2)
    def _():
        for k in range(CHUNKS):
            halo[k, 2 * level_lags : lags - 1] = jnp.zeros(
                (lags - 1 - 2 * level_lags, inputs, piece), jnp.bfloat16)

    @pl.when(level == levels - 1)
    def _():
        for k in range(CHUNKS):
            halo[k, level_lags : 2 * level_lags] = jnp.zeros(
                (level_lags, inputs, piece), jnp.bfloat16)

    def own_down(k):
        for s in (1, 2, 3):
            spread_in(k, s).wait_recv()

            @pl.when(level > 0)
            def _():
                down(k, s).start()

    def pass_on(k):
        @pl.when(level < levels - 1)
        def _():
            for s in range(TEAM):
                down(k, s).wait_recv()

            @pl.when(level > 0)
            def _():
                forward(k).start()

    def compute(k):
        keep(k).wait()

        @pl.when(level < levels - 2)
        def _():
            forward(k).wait_recv()

        window = halo[k].reshape(lags * inputs, piece)
        sketch = jnp.dot(weights[...], window, preferred_element_type=jnp.float32)
        sk[k] = sketch.reshape(level_lags, rank, piece)
        for s in (2, 3, 1):
            give_back(k, s).start()
        own[place, k] = sk[k, pl.ds(per * place, per)]
        wide = jnp.concatenate([sketch[i * rank : (i + 1) * rank] for i in range(level_lags)], axis=1)
        local = lax.dot_general(wide, wide, NT, precision=HIGH, preferred_element_type=jnp.float32)
        gram_acc[:, :rank] = local if k == 0 else gram_acc[:, :rank] + local
        if k == CHUNKS - 1:
            share_gram()
        parts = split3(sketch)
        product = sum(
            lax.dot_general(part, window, NT, preferred_element_type=jnp.float32)
            for part in reversed(parts)
        )
        corr[...] = product if k == 0 else corr[...] + product

    def gram_to(step):
        other = lax.rem(me + step, count)
        return remote(pack, gbuf.at[me], m0s.at[step], m0r.at[me], other)

    def gram_in(step):
        other = lax.rem(me + step, count)
        return remote(pack, gbuf.at[other], m0s.at[step], m0r.at[other], other)

    def share_gram():
        packed = gram_acc[0:8, :]
        for b in range(1, rank // 8):
            packed = packed + pltpu.roll(gram_acc[8 * b : 8 * b + 8, :], b * rank, 1)
        pack[...] = packed

        @pl.loop(1, count)
        def _(step):
            gram_to(step).start()

        gbuf[me] = packed

    own_down(0)
    own_down(1)
    gram_acc[...] = jnp.zeros_like(gram_acc)
    turned = omega_ref[...].astype(jnp.float32) * 0.25
    band = jnp.concatenate(
        [turned, jnp.zeros((rank, weights.shape[1] - turned.shape[1]), jnp.float32)], axis=1)
    for i in range(level_lags):
        row = band if i == 0 else pltpu.roll(band, i * inputs, 1)
        weights[i * rank : (i + 1) * rank, :] = row.astype(jnp.bfloat16)
    pass_on(0)
    for k in range(2, CHUNKS):
        own_down(k)
        pass_on(k - 1)
        if k > 2:
            compute(k - 3)
    compute(CHUNKS - 3)
    pass_on(CHUNKS - 1)
    compute(CHUNKS - 2)
    compute(CHUNKS - 1)

    folded = corr[0:rank, : J * inputs]
    for i in range(1, level_lags):
        turned_back = pltpu.roll(corr[i * rank : (i + 1) * rank, :], lags * inputs - i * inputs, 1)
        folded = folded + turned_back[:, : J * inputs]
    tiles_across = J * inputs // 128
    tiles = (rank // 8) * tiles_across
    for d in range(count):
        if d < tiles:
            a, b = divmod(d, tiles_across)
            msg[d] = folded[8 * a : 8 * a + 8, 128 * b : 128 * b + 128]
        else:
            msg[d] = jnp.zeros((8, 128), jnp.float32)

    def partial(step):
        other = lax.rem(me + step, count)
        return remote(msg.at[other], rbuf.at[me], m1s.at[step], m1r.at[me], other)

    def partial_in(step):
        other = lax.rem(me + step, count)
        return remote(msg.at[other], rbuf.at[other], m1s.at[step], m1r.at[other], other)

    def whole(step):
        other = lax.rem(me + step, count)
        return remote(kred, kfin.at[me], m2s.at[step], m2r.at[me], other)

    def whole_in(step):
        other = lax.rem(me + step, count)
        return remote(kred, kfin.at[other], m2s.at[step], m2r.at[other], other)

    @pl.loop(1, count)
    def _(step):
        partial(step).start()

    rbuf[me] = msg[me]

    @pl.loop(1, count)
    def _(step):
        gram_in(step).wait_recv()

    @pl.loop(1, count)
    def _(step):
        partial_in(step).wait_recv()

    product = rbuf[0]
    total = gbuf[0]
    for d in range(1, count):
        product = product + rbuf[d]
        total = total + gbuf[d]
    kred[...] = product
    kfin[me] = product

    @pl.loop(1, count)
    def _(step):
        whole(step).start()

    lanes = lax.broadcasted_iota(jnp.int32, (8, 128), 1)
    blocks = []
    for b in range(rank // 8):
        block = total if b == 0 else pltpu.roll(total, 128 - b * rank, 1)
        blocks.append(jnp.where(lanes < rank, block, 0.0))
    inverse = inverse_factor(jnp.concatenate(blocks, axis=0) * (1.0 / total_rows))

    for k in range(CHUNKS):
        for s in range(1, TEAM):
            give_back_in(k, s).wait_recv()
    for q in range(TEAM):
        for k in range(CHUNKS):
            for g in range(per):
                basis_ref[g, :, q * quarter + k * piece : q * quarter + (k + 1) * piece] = jnp.dot(
                    inverse, own[q, k, g], precision=HIGH, preferred_element_type=jnp.float32)

    @pl.loop(1, count)
    def _(step):
        whole_in(step).wait_recv()

    summed = jnp.concatenate(
        [jnp.concatenate([kfin[a * tiles_across + b] for b in range(tiles_across)], axis=1)
         for a in range(rank // 8)], axis=0)
    coupled_ref[...] = jnp.dot(
        inverse, summed, precision=HIGH, preferred_element_type=jnp.float32
    ) * (1.0 / math.sqrt(total_rows))

    for k in range(CHUNKS):
        for s in range(1, TEAM):
            spread(k, s).wait_send()
            give_back(k, s).wait_send()

    @pl.when(level > 0)
    def _():
        for k in range(CHUNKS):
            for s in range(TEAM):
                down(k, s).wait_send()

    @pl.when(jnp.logical_and(level > 0, level < levels - 1))
    def _():
        for k in range(CHUNKS):
            forward(k).wait_send()

    @pl.loop(1, count)
    def _(step):
        gram_to(step).wait_send()
        partial(step).wait_send()
        whole(step).wait_send()


def per_device(count, markov, omega):
    per, inputs, width = markov.shape
    rank = omega.shape[1]
    piece = width // TEAM // CHUNKS
    level_lags = per * TEAM
    lags = level_lags + J
    dma = pltpu.SemaphoreType.DMA
    vmem = pl.BlockSpec(memory_space=pltpu.VMEM)
    return pl.pallas_call(
        functools.partial(kernel, count),
        out_shape=(
            jax.ShapeDtypeStruct((per, rank, width), jnp.float32),
            jax.ShapeDtypeStruct((rank, J * inputs), jnp.float32),
        ),
        in_specs=[pl.BlockSpec(memory_space=pltpu.HBM), vmem],
        out_specs=(vmem, vmem),
        scratch_shapes=[
            pltpu.VMEM((CHUNKS, lags, inputs, piece), jnp.bfloat16),
            pltpu.VMEM((level_lags * rank, lags * inputs), jnp.bfloat16),
            pltpu.VMEM((CHUNKS, level_lags, rank, piece), jnp.float32),
            pltpu.VMEM((TEAM, CHUNKS, per, rank, piece), jnp.float32),
            pltpu.VMEM((level_lags * rank, lags * inputs), jnp.float32),
            pltpu.VMEM((rank, 128), jnp.float32),
            pltpu.VMEM((8, 128), jnp.float32),
            pltpu.VMEM((count, 8, 128), jnp.float32),
            pltpu.VMEM((count, 8, 128), jnp.float32),
            pltpu.VMEM((count, 8, 128), jnp.float32),
            pltpu.VMEM((8, 128), jnp.float32),
            pltpu.VMEM((count, 8, 128), jnp.float32),
            dma((CHUNKS,)),
            dma((CHUNKS, TEAM)), dma((CHUNKS, TEAM)), dma((CHUNKS, TEAM)), dma((CHUNKS, TEAM)),
            dma((CHUNKS,)), dma((CHUNKS,)), dma((CHUNKS, TEAM)), dma((CHUNKS, TEAM)),
            dma((count,)), dma((count,)), dma((count,)), dma((count,)), dma((count,)), dma((count,)),
        ],
        compiler_params=pltpu.CompilerParams(
            collective_id=0, has_side_effects=True, vmem_limit_bytes=40 * 2**20
        ),
        cost_estimate=pl.CostEstimate(flops=6 * 10**9, bytes_accessed=8 * 2**20, transcendentals=0),
    )(markov, omega.T)


def solution(mesh):
    return jax.shard_map(
        functools.partial(per_device, mesh.shape["lag"]),
        mesh=mesh,
        in_specs=(P(("group", "lag"), None, None), P()),
        out_specs=(P(("group", "lag"), None, None), P("group", None)),
        check_vma=False,
    )
```

```python
import functools
import math

import jax
import jax.numpy as jnp
from jax import lax
from jax.experimental import pallas as pl
from jax.experimental.pallas import tpu as pltpu
from jax.sharding import PartitionSpec as P

J = 16
TEAM = 4
CHUNKS = 8
HIGH = lax.Precision.HIGHEST
NT = (((1,), (1,)), ((), ()))


def split3(value):
    high = value.astype(jnp.bfloat16)
    rest = value - high.astype(jnp.float32)
    middle = rest.astype(jnp.bfloat16)
    low = (rest - middle.astype(jnp.float32)).astype(jnp.bfloat16)
    return high, middle, low


def inverse_factor(gram):
    size = gram.shape[0]
    rows = lax.broadcasted_iota(jnp.int32, (size, 128), 0)
    lanes = lax.broadcasted_iota(jnp.int32, (size, 128), 1)
    work = gram + jnp.where(lanes == rows + size, 1.0, 0.0)
    for step in range(size):
        pivot_row = work[step : step + 1, :]
        pivot = pivot_row[:, step : step + 1]
        scale = lax.rsqrt(pivot)
        scale = scale * (1.5 - 0.5 * pivot * scale * scale)
        unit_row = pivot_row * scale
        column = work[:, step : step + 1] * scale
        work = jnp.where(
            rows > step, work - column * unit_row, jnp.where(rows == step, unit_row, work)
        )
    return pltpu.roll(work, 128 - size, 1)[:, :size]


def kernel(count, x_ref, omega_ref, own, inverse_ref, summed_ref, halo, weights, sk, corr, gram_acc,
           pack, gbuf, msg, rbuf, kred, kfin, xs, p1s, p1r, dns, dnr, fws, fwr, srs, srr, os, m0s, m0r, m1s, m1r,
           m2s, m2r):
    per, inputs, width = x_ref.shape
    rank = omega_ref.shape[0]
    quarter = width // TEAM
    piece = quarter // CHUNKS
    level_lags = per * TEAM
    reach = J - 1
    lags = halo.shape[1]
    levels = count // TEAM
    total_rows = count * per * width
    me = lax.axis_index("lag")
    level, place = me // TEAM, me % TEAM
    mates = [place, place + 1 - 2 * (place % 2), (place + 2) % TEAM, TEAM - 1 - place]
    below = lax.rem(me + count - TEAM, count)

    barrier = pltpu.get_barrier_semaphore()

    @pl.loop(1, count)
    def _(step):
        pl.semaphore_signal(barrier, inc=1, device_id={"lag": lax.rem(me + step, count)},
                            device_id_type=pl.DeviceIdType.MESH)

    pl.semaphore_wait(barrier, count - 1)

    def remote(src, dst, send, recv, target):
        return pltpu.make_async_remote_copy(
            src_ref=src, dst_ref=dst, send_sem=send, recv_sem=recv,
            device_id={"lag": target}, device_id_type=pl.DeviceIdType.MESH)

    def columns(who, k):
        return pl.ds(pl.multiple_of(who * quarter + k * piece, 128), piece)

    def spread(k, s):
        mate = mates[s]
        return remote(x_ref.at[:, :, columns(mate, k)], halo.at[k, pl.ds(per * place, per)],
                      p1s.at[k, s], p1r.at[k, place], level * TEAM + mate)

    def spread_in(k, s):
        mate = mates[s]
        dst = halo.at[k, pl.ds(per * mate, per)]
        return remote(dst, dst, p1s.at[k, s], p1r.at[k, mate], level * TEAM + mate)

    def down(k, s):
        mate = mates[s]
        src = x_ref.at[:, :, columns(place, k)] if s == 0 else halo.at[k, pl.ds(per * mate, per)]
        return remote(src, halo.at[k, pl.ds(level_lags + per * mate, per)],
                      dns.at[k, s], dnr.at[k, mate], below)

    def forward(k):
        return remote(halo.at[k, pl.ds(level_lags, reach - level_lags)],
                      halo.at[k, pl.ds(2 * level_lags, reach - level_lags)],
                      fws.at[k], fwr.at[k], below)

    def give_back(k, s):
        mate = mates[s]
        return remote(sk.at[k, pl.ds(per * mate, per)], own.at[place, k],
                      srs.at[k, s], srr.at[k, place], level * TEAM + mate)

    def give_back_in(k, s):
        mate = mates[s]
        return remote(own.at[mate, k], own.at[mate, k], srs.at[k, s], srr.at[k, mate],
                      level * TEAM + mate)

    def keep(k):
        return pltpu.make_async_copy(x_ref.at[:, :, columns(place, k)],
                                     halo.at[k, pl.ds(per * place, per)], xs.at[k])

    def stay(k):
        return pltpu.make_async_copy(sk.at[k, pl.ds(per * place, per)], own.at[place, k], os.at[k])

    for k in range(CHUNKS):
        for s in (2, 3, 1):
            spread(k, s).start()

        @pl.when(level > 0)
        def _():
            down(k, 0).start()

        keep(k).start()

    for k in range(CHUNKS):
        halo[k, lags - 1] = jnp.zeros((inputs, piece), jnp.bfloat16)

    @pl.when(level >= levels - 2)
    def _():
        for k in range(CHUNKS):
            halo[k, 2 * level_lags : lags - 1] = jnp.zeros(
                (lags - 1 - 2 * level_lags, inputs, piece), jnp.bfloat16)

    @pl.when(level == levels - 1)
    def _():
        for k in range(CHUNKS):
            halo[k, level_lags : 2 * level_lags] = jnp.zeros(
                (level_lags, inputs, piece), jnp.bfloat16)

    def own_down(k):
        for s in (1, 2, 3):
            spread_in(k, s).wait_recv()

            @pl.when(level > 0)
            def _():
                down(k, s).start()

    def pass_on(k):
        @pl.when(level < levels - 1)
        def _():
            for s in range(TEAM):
                down(k, s).wait_recv()

            @pl.when(level > 0)
            def _():
                forward(k).start()

    def compute(k):
        keep(k).wait()

        @pl.when(level < levels - 2)
        def _():
            forward(k).wait_recv()

        window = halo[k].reshape(lags * inputs, piece)
        sketch = jnp.dot(weights[...], window, preferred_element_type=jnp.float32)
        sk[k] = sketch.reshape(level_lags, rank, piece)
        for s in (2, 3, 1):
            give_back(k, s).start()
        stay(k).start()
        wide = jnp.concatenate([sketch[i * rank : (i + 1) * rank] for i in range(level_lags)], axis=1)
        local = lax.dot_general(wide, wide, NT, precision=HIGH, preferred_element_type=jnp.float32)
        gram_acc[:, :rank] = local if k == 0 else gram_acc[:, :rank] + local
        if k == CHUNKS - 1:
            share_gram()
        parts = split3(sketch)
        product = sum(
            lax.dot_general(part, window, NT, preferred_element_type=jnp.float32)
            for part in reversed(parts)
        )
        corr[...] = product if k == 0 else corr[...] + product

    def gram_to(step):
        other = lax.rem(me + step, count)
        return remote(pack, gbuf.at[me], m0s.at[step], m0r.at[me], other)

    def gram_in(step):
        other = lax.rem(me + step, count)
        return remote(pack, gbuf.at[other], m0s.at[step], m0r.at[other], other)

    def share_gram():
        packed = gram_acc[0:8, :]
        for b in range(1, rank // 8):
            packed = packed + pltpu.roll(gram_acc[8 * b : 8 * b + 8, :], b * rank, 1)
        pack[...] = packed

        @pl.loop(1, count)
        def _(step):
            gram_to(step).start()

        gbuf[me] = packed

    own_down(0)
    own_down(1)
    gram_acc[...] = jnp.zeros_like(gram_acc)
    turned = omega_ref[...].astype(jnp.float32) * 0.25
    band = jnp.concatenate(
        [turned, jnp.zeros((rank, weights.shape[1] - turned.shape[1]), jnp.float32)], axis=1)
    for i in range(level_lags):
        row = band if i == 0 else pltpu.roll(band, i * inputs, 1)
        weights[i * rank : (i + 1) * rank, :] = row.astype(jnp.bfloat16)
    pass_on(0)
    for k in range(2, CHUNKS):
        own_down(k)
        pass_on(k - 1)
        if k > 2:
            compute(k - 3)
    compute(CHUNKS - 3)
    pass_on(CHUNKS - 1)
    compute(CHUNKS - 2)
    compute(CHUNKS - 1)

    folded = corr[0:rank, : J * inputs]
    for i in range(1, level_lags):
        turned_back = pltpu.roll(corr[i * rank : (i + 1) * rank, :], lags * inputs - i * inputs, 1)
        folded = folded + turned_back[:, : J * inputs]
    tiles_across = J * inputs // 128
    tiles = (rank // 8) * tiles_across
    for d in range(count):
        if d < tiles:
            a, b = divmod(d, tiles_across)
            msg[d] = folded[8 * a : 8 * a + 8, 128 * b : 128 * b + 128]
        else:
            msg[d] = jnp.zeros((8, 128), jnp.float32)

    def partial(step):
        other = lax.rem(me + step, count)
        return remote(msg.at[other], rbuf.at[me], m1s.at[step], m1r.at[me], other)

    def partial_in(step):
        other = lax.rem(me + step, count)
        return remote(msg.at[other], rbuf.at[other], m1s.at[step], m1r.at[other], other)

    def whole(step):
        other = lax.rem(me + step, count)
        return remote(kred, kfin.at[me], m2s.at[step], m2r.at[me], other)

    def whole_in(step):
        other = lax.rem(me + step, count)
        return remote(kred, kfin.at[other], m2s.at[step], m2r.at[other], other)

    @pl.loop(1, count)
    def _(step):
        partial(step).start()

    rbuf[me] = msg[me]

    @pl.loop(1, count)
    def _(step):
        gram_in(step).wait_recv()

    @pl.loop(1, count)
    def _(step):
        partial_in(step).wait_recv()

    product = rbuf[0]
    total = gbuf[0]
    for d in range(1, count):
        product = product + rbuf[d]
        total = total + gbuf[d]
    kred[...] = product
    kfin[me] = product

    @pl.loop(1, count)
    def _(step):
        whole(step).start()

    lanes = lax.broadcasted_iota(jnp.int32, (8, 128), 1)
    blocks = []
    for b in range(rank // 8):
        block = total if b == 0 else pltpu.roll(total, 128 - b * rank, 1)
        blocks.append(jnp.where(lanes < rank, block, 0.0))
    inverse = inverse_factor(jnp.concatenate(blocks, axis=0) * (1.0 / total_rows))

    inverse_ref[...] = inverse

    @pl.loop(1, count)
    def _(step):
        whole_in(step).wait_recv()

    summed_ref[...] = jnp.concatenate(
        [jnp.concatenate([kfin[a * tiles_across + b] for b in range(tiles_across)], axis=1)
         for a in range(rank // 8)], axis=0)

    for k in range(CHUNKS):
        for s in range(1, TEAM):
            give_back_in(k, s).wait_recv()
        stay(k).wait()

    for k in range(CHUNKS):
        for s in range(1, TEAM):
            spread(k, s).wait_send()
            give_back(k, s).wait_send()

    @pl.when(level > 0)
    def _():
        for k in range(CHUNKS):
            for s in range(TEAM):
                down(k, s).wait_send()

    @pl.when(jnp.logical_and(level > 0, level < levels - 1))
    def _():
        for k in range(CHUNKS):
            forward(k).wait_send()

    @pl.loop(1, count)
    def _(step):
        gram_to(step).wait_send()
        partial(step).wait_send()
        whole(step).wait_send()


def whiten_kernel(total_rows, inverse_ref, summed_ref, own_ref, basis_ref, coupled_ref):
    _, chunks, per, _, piece = own_ref.shape
    inverse = inverse_ref[...]

    @pl.when(pl.program_id(0) == 0)
    def _():
        coupled_ref[...] = jnp.dot(
            inverse, summed_ref[...], precision=HIGH, preferred_element_type=jnp.float32
        ) * (1.0 / math.sqrt(total_rows))

    for k in range(chunks):
        for g in range(per):
            basis_ref[g, :, k * piece : (k + 1) * piece] = jnp.dot(
                inverse, own_ref[0, k, g], precision=HIGH, preferred_element_type=jnp.float32)


def per_device(count, markov, omega):
    per, inputs, width = markov.shape
    rank = omega.shape[1]
    piece = width // TEAM // CHUNKS
    level_lags = per * TEAM
    lags = level_lags + J
    dma = pltpu.SemaphoreType.DMA
    vmem = pl.BlockSpec(memory_space=pltpu.VMEM)
    own, inverse, summed = pl.pallas_call(
        functools.partial(kernel, count),
        out_shape=(
            jax.ShapeDtypeStruct((TEAM, CHUNKS, per, rank, piece), jnp.float32),
            jax.ShapeDtypeStruct((rank, rank), jnp.float32),
            jax.ShapeDtypeStruct((rank, J * inputs), jnp.float32),
        ),
        in_specs=[pl.BlockSpec(memory_space=pl.ANY), vmem],
        out_specs=(pl.BlockSpec(memory_space=pl.ANY), vmem, vmem),
        scratch_shapes=[
            pltpu.VMEM((CHUNKS, lags, inputs, piece), jnp.bfloat16),
            pltpu.VMEM((level_lags * rank, lags * inputs), jnp.bfloat16),
            pltpu.VMEM((CHUNKS, level_lags, rank, piece), jnp.float32),
            pltpu.VMEM((level_lags * rank, lags * inputs), jnp.float32),
            pltpu.VMEM((rank, 128), jnp.float32),
            pltpu.VMEM((8, 128), jnp.float32),
            pltpu.VMEM((count, 8, 128), jnp.float32),
            pltpu.VMEM((count, 8, 128), jnp.float32),
            pltpu.VMEM((count, 8, 128), jnp.float32),
            pltpu.VMEM((8, 128), jnp.float32),
            pltpu.VMEM((count, 8, 128), jnp.float32),
            dma((CHUNKS,)),
            dma((CHUNKS, TEAM)), dma((CHUNKS, TEAM)), dma((CHUNKS, TEAM)), dma((CHUNKS, TEAM)),
            dma((CHUNKS,)), dma((CHUNKS,)), dma((CHUNKS, TEAM)), dma((CHUNKS, TEAM)), dma((CHUNKS,)),
            dma((count,)), dma((count,)), dma((count,)), dma((count,)), dma((count,)), dma((count,)),
        ],
        compiler_params=pltpu.CompilerParams(
            collective_id=0, has_side_effects=True, vmem_limit_bytes=60 * 2**20
        ),
        cost_estimate=pl.CostEstimate(flops=6 * 10**9, bytes_accessed=8 * 2**20, transcendentals=0),
    )(markov, omega.T)
    small = lambda shape: pl.BlockSpec(shape, lambda q: (0, 0))
    return pl.pallas_call(
        functools.partial(whiten_kernel, count * per * width),
        grid=(TEAM,),
        out_shape=(
            jax.ShapeDtypeStruct((per, rank, width), jnp.float32),
            jax.ShapeDtypeStruct((rank, J * inputs), jnp.float32),
        ),
        in_specs=[
            small((rank, rank)),
            small((rank, J * inputs)),
            pl.BlockSpec((1, CHUNKS, per, rank, piece), lambda q: (q, 0, 0, 0, 0)),
        ],
        out_specs=(
            pl.BlockSpec((per, rank, width // TEAM), lambda q: (0, 0, q)),
            small((rank, J * inputs)),
        ),
        compiler_params=pltpu.CompilerParams(vmem_limit_bytes=60 * 2**20),
    )(inverse, summed, own)


def solution(mesh):
    return jax.shard_map(
        functools.partial(per_device, mesh.shape["lag"]),
        mesh=mesh,
        in_specs=(P(("group", "lag"), None, None), P()),
        out_specs=(P(("group", "lag"), None, None), P("group", None)),
        check_vma=False,
    )
```

```python
import functools
import math

import jax
import jax.numpy as jnp
from jax import lax
from jax.experimental import pallas as pl
from jax.experimental.pallas import tpu as pltpu
from jax.sharding import PartitionSpec as P

J = 16
TEAM = 4
CHUNKS = 8
HIGH = lax.Precision.HIGHEST
NT = (((1,), (1,)), ((), ()))


def split3(value):
    high = value.astype(jnp.bfloat16)
    rest = value - high.astype(jnp.float32)
    middle = rest.astype(jnp.bfloat16)
    low = (rest - middle.astype(jnp.float32)).astype(jnp.bfloat16)
    return high, middle, low


def inverse_factor(gram):
    size = gram.shape[0]
    rows = lax.broadcasted_iota(jnp.int32, (size, 128), 0)
    lanes = lax.broadcasted_iota(jnp.int32, (size, 128), 1)
    work = gram + jnp.where(lanes == rows + size, 1.0, 0.0)
    for step in range(size):
        pivot_row = work[step : step + 1, :]
        pivot = pivot_row[:, step : step + 1]
        scale = lax.rsqrt(pivot)
        scale = scale * (1.5 - 0.5 * pivot * scale * scale)
        unit_row = pivot_row * scale
        column = work[:, step : step + 1] * scale
        work = jnp.where(
            rows > step, work - column * unit_row, jnp.where(rows == step, unit_row, work)
        )
    return pltpu.roll(work, 128 - size, 1)[:, :size]


def kernel(count, x_ref, omega_ref, basis_ref, coupled_ref, halo, weights, sk, own, corr, gram_acc,
           pack, gbuf, msg, rbuf, kred, kfin, xs, p1s, p1r, dns, dnr, fws, fwr, srs, srr, m0s, m0r, m1s, m1r,
           m2s, m2r):
    per, inputs, width = x_ref.shape
    rank = omega_ref.shape[0]
    quarter = width // TEAM
    piece = quarter // CHUNKS
    level_lags = per * TEAM
    reach = J - 1
    lags = halo.shape[1]
    levels = count // TEAM
    total_rows = count * per * width
    me = lax.axis_index("lag")
    level, place = me // TEAM, me % TEAM
    mates = [place, place + 1 - 2 * (place % 2), (place + 2) % TEAM, TEAM - 1 - place]
    below = lax.rem(me + count - TEAM, count)

    barrier = pltpu.get_barrier_semaphore()

    @pl.loop(1, count)
    def _(step):
        pl.semaphore_signal(barrier, inc=1, device_id={"lag": lax.rem(me + step, count)},
                            device_id_type=pl.DeviceIdType.MESH)

    pl.semaphore_wait(barrier, count - 1)

    def remote(src, dst, send, recv, target):
        return pltpu.make_async_remote_copy(
            src_ref=src, dst_ref=dst, send_sem=send, recv_sem=recv,
            device_id={"lag": target}, device_id_type=pl.DeviceIdType.MESH)

    def columns(who, k):
        return pl.ds(pl.multiple_of(who * quarter + k * piece, 128), piece)

    def spread(k, s):
        mate = mates[s]
        return remote(x_ref.at[:, :, columns(mate, k)], halo.at[k, pl.ds(per * place, per)],
                      p1s.at[k, s], p1r.at[k, place], level * TEAM + mate)

    def spread_in(k, s):
        mate = mates[s]
        dst = halo.at[k, pl.ds(per * mate, per)]
        return remote(dst, dst, p1s.at[k, s], p1r.at[k, mate], level * TEAM + mate)

    def down(k, s):
        mate = mates[s]
        src = x_ref.at[:, :, columns(place, k)] if s == 0 else halo.at[k, pl.ds(per * mate, per)]
        return remote(src, halo.at[k, pl.ds(level_lags + per * mate, per)],
                      dns.at[k, s], dnr.at[k, mate], below)

    def forward(k):
        return remote(halo.at[k, pl.ds(level_lags, reach - level_lags)],
                      halo.at[k, pl.ds(2 * level_lags, reach - level_lags)],
                      fws.at[k], fwr.at[k], below)

    def give_back(k, s):
        mate = mates[s]
        return remote(sk.at[k, pl.ds(per * mate, per)], own.at[place, k],
                      srs.at[k, s], srr.at[k, place], level * TEAM + mate)

    def give_back_in(k, s):
        mate = mates[s]
        return remote(own.at[mate, k], own.at[mate, k], srs.at[k, s], srr.at[k, mate],
                      level * TEAM + mate)

    def keep(k):
        return pltpu.make_async_copy(x_ref.at[:, :, columns(place, k)],
                                     halo.at[k, pl.ds(per * place, per)], xs.at[k])

    for k in range(CHUNKS):
        for s in (2, 3, 1):
            spread(k, s).start()

        @pl.when(level > 0)
        def _():
            down(k, 0).start()

        keep(k).start()

    for k in range(CHUNKS):
        halo[k, lags - 1] = jnp.zeros((inputs, piece), jnp.bfloat16)

    @pl.when(level >= levels - 2)
    def _():
        for k in range(CHUNKS):
            halo[k, 2 * level_lags : lags - 1] = jnp.zeros(
                (lags - 1 - 2 * level_lags, inputs, piece), jnp.bfloat16)

    @pl.when(level == levels - 1)
    def _():
        for k in range(CHUNKS):
            halo[k, level_lags : 2 * level_lags] = jnp.zeros(
                (level_lags, inputs, piece), jnp.bfloat16)

    def own_down(k):
        for s in (1, 2, 3):
            spread_in(k, s).wait_recv()

            @pl.when(level > 0)
            def _():
                down(k, s).start()

    def pass_on(k):
        @pl.when(level < levels - 1)
        def _():
            for s in range(TEAM):
                down(k, s).wait_recv()

            @pl.when(level > 0)
            def _():
                forward(k).start()

    def compute(k):
        keep(k).wait()

        @pl.when(level < levels - 2)
        def _():
            forward(k).wait_recv()

        window = halo[k].reshape(lags * inputs, piece)
        sketch = jnp.dot(weights[...], window, preferred_element_type=jnp.float32)
        sk[k] = sketch.reshape(level_lags, rank, piece)
        for s in (2, 3, 1):
            give_back(k, s).start()
        own[place, k] = sk[k, pl.ds(per * place, per)]
        wide = jnp.concatenate([sketch[i * rank : (i + 1) * rank] for i in range(level_lags)], axis=1)
        local = lax.dot_general(wide, wide, NT, precision=HIGH, preferred_element_type=jnp.float32)
        gram_acc[:, :rank] = local if k == 0 else gram_acc[:, :rank] + local
        if k == CHUNKS - 1:
            share_gram()
        parts = split3(sketch)
        product = sum(
            lax.dot_general(part, window, NT, preferred_element_type=jnp.float32)
            for part in reversed(parts)
        )
        corr[...] = product if k == 0 else corr[...] + product

    def gram_to(step):
        other = lax.rem(me + step, count)
        return remote(pack, gbuf.at[me], m0s.at[step], m0r.at[me], other)

    def gram_in(step):
        other = lax.rem(me + step, count)
        return remote(pack, gbuf.at[other], m0s.at[step], m0r.at[other], other)

    def share_gram():
        packed = gram_acc[0:8, :]
        for b in range(1, rank // 8):
            packed = packed + pltpu.roll(gram_acc[8 * b : 8 * b + 8, :], b * rank, 1)
        pack[...] = packed

        @pl.loop(1, count)
        def _(step):
            gram_to(step).start()

        gbuf[me] = packed

    own_down(0)
    own_down(1)
    gram_acc[...] = jnp.zeros_like(gram_acc)
    turned = omega_ref[...].astype(jnp.float32) * 0.25
    band = jnp.concatenate(
        [turned, jnp.zeros((rank, weights.shape[1] - turned.shape[1]), jnp.float32)], axis=1)
    for i in range(level_lags):
        row = band if i == 0 else pltpu.roll(band, i * inputs, 1)
        weights[i * rank : (i + 1) * rank, :] = row.astype(jnp.bfloat16)
    pass_on(0)
    for k in range(2, CHUNKS):
        own_down(k)
        pass_on(k - 1)
        if k > 2:
            compute(k - 3)
    compute(CHUNKS - 3)
    pass_on(CHUNKS - 1)
    compute(CHUNKS - 2)
    compute(CHUNKS - 1)

    folded = corr[0:rank, : J * inputs]
    for i in range(1, level_lags):
        turned_back = pltpu.roll(corr[i * rank : (i + 1) * rank, :], lags * inputs - i * inputs, 1)
        folded = folded + turned_back[:, : J * inputs]
    tiles_across = J * inputs // 128
    tiles = (rank // 8) * tiles_across
    for d in range(count):
        if d < tiles:
            a, b = divmod(d, tiles_across)
            msg[d] = folded[8 * a : 8 * a + 8, 128 * b : 128 * b + 128]
        else:
            msg[d] = jnp.zeros((8, 128), jnp.float32)

    def partial(step):
        other = lax.rem(me + step, count)
        return remote(msg.at[other], rbuf.at[me], m1s.at[step], m1r.at[me], other)

    def partial_in(step):
        other = lax.rem(me + step, count)
        return remote(msg.at[other], rbuf.at[other], m1s.at[step], m1r.at[other], other)

    def whole(step):
        other = lax.rem(me + step, count)
        return remote(kred, kfin.at[me], m2s.at[step], m2r.at[me], other)

    def whole_in(step):
        other = lax.rem(me + step, count)
        return remote(kred, kfin.at[other], m2s.at[step], m2r.at[other], other)

    @pl.loop(1, count)
    def _(step):
        partial(step).start()

    rbuf[me] = msg[me]

    @pl.loop(1, count)
    def _(step):
        gram_in(step).wait_recv()

    @pl.loop(1, count)
    def _(step):
        partial_in(step).wait_recv()

    product = rbuf[0]
    total = gbuf[0]
    for d in range(1, count):
        product = product + rbuf[d]
        total = total + gbuf[d]
    kred[...] = product
    kfin[me] = product

    @pl.loop(1, count)
    def _(step):
        whole(step).start()

    lanes = lax.broadcasted_iota(jnp.int32, (8, 128), 1)
    blocks = []
    for b in range(rank // 8):
        block = total if b == 0 else pltpu.roll(total, 128 - b * rank, 1)
        blocks.append(jnp.where(lanes < rank, block, 0.0))
    inverse = inverse_factor(jnp.concatenate(blocks, axis=0) * (1.0 / total_rows))

    for k in range(CHUNKS):
        for s in range(1, TEAM):
            give_back_in(k, s).wait_recv()
    for q in range(TEAM):
        for k in range(CHUNKS):
            for g in range(per):
                basis_ref[g, :, q * quarter + k * piece : q * quarter + (k + 1) * piece] = jnp.dot(
                    inverse, own[q, k, g], precision=HIGH, preferred_element_type=jnp.float32)

    @pl.loop(1, count)
    def _(step):
        whole_in(step).wait_recv()

    summed = jnp.concatenate(
        [jnp.concatenate([kfin[a * tiles_across + b] for b in range(tiles_across)], axis=1)
         for a in range(rank // 8)], axis=0)
    coupled_ref[...] = jnp.dot(
        inverse, summed, precision=HIGH, preferred_element_type=jnp.float32
    ) * (1.0 / math.sqrt(total_rows))

    for k in range(CHUNKS):
        for s in range(1, TEAM):
            spread(k, s).wait_send()
            give_back(k, s).wait_send()

    @pl.when(level > 0)
    def _():
        for k in range(CHUNKS):
            for s in range(TEAM):
                down(k, s).wait_send()

    @pl.when(jnp.logical_and(level > 0, level < levels - 1))
    def _():
        for k in range(CHUNKS):
            forward(k).wait_send()

    @pl.loop(1, count)
    def _(step):
        gram_to(step).wait_send()
        partial(step).wait_send()
        whole(step).wait_send()


def per_device(count, markov, omega):
    per, inputs, width = markov.shape
    rank = omega.shape[1]
    piece = width // TEAM // CHUNKS
    level_lags = per * TEAM
    lags = level_lags + J
    dma = pltpu.SemaphoreType.DMA
    vmem = pl.BlockSpec(memory_space=pltpu.VMEM)
    return pl.pallas_call(
        functools.partial(kernel, count),
        out_shape=(
            jax.ShapeDtypeStruct((per, rank, width), jnp.float32),
            jax.ShapeDtypeStruct((rank, J * inputs), jnp.float32),
        ),
        in_specs=[pl.BlockSpec(memory_space=pltpu.HBM), vmem],
        out_specs=(vmem, vmem),
        scratch_shapes=[
            pltpu.VMEM((CHUNKS, lags, inputs, piece), jnp.bfloat16),
            pltpu.VMEM((level_lags * rank, lags * inputs), jnp.bfloat16),
            pltpu.VMEM((CHUNKS, level_lags, rank, piece), jnp.float32),
            pltpu.VMEM((TEAM, CHUNKS, per, rank, piece), jnp.float32),
            pltpu.VMEM((level_lags * rank, lags * inputs), jnp.float32),
            pltpu.VMEM((rank, 128), jnp.float32),
            pltpu.VMEM((8, 128), jnp.float32),
            pltpu.VMEM((count, 8, 128), jnp.float32),
            pltpu.VMEM((count, 8, 128), jnp.float32),
            pltpu.VMEM((count, 8, 128), jnp.float32),
            pltpu.VMEM((8, 128), jnp.float32),
            pltpu.VMEM((count, 8, 128), jnp.float32),
            dma((CHUNKS,)),
            dma((CHUNKS, TEAM)), dma((CHUNKS, TEAM)), dma((CHUNKS, TEAM)), dma((CHUNKS, TEAM)),
            dma((CHUNKS,)), dma((CHUNKS,)), dma((CHUNKS, TEAM)), dma((CHUNKS, TEAM)),
            dma((count,)), dma((count,)), dma((count,)), dma((count,)), dma((count,)), dma((count,)),
        ],
        compiler_params=pltpu.CompilerParams(
            collective_id=0, has_side_effects=True, vmem_limit_bytes=60 * 2**20
        ),
        cost_estimate=pl.CostEstimate(flops=6 * 10**9, bytes_accessed=8 * 2**20, transcendentals=0),
    )(markov, omega.T)


def solution(mesh):
    return jax.shard_map(
        functools.partial(per_device, mesh.shape["lag"]),
        mesh=mesh,
        in_specs=(P(("group", "lag"), None, None), P()),
        out_specs=(P(("group", "lag"), None, None), P("group", None)),
        check_vma=False,
    )
```

```python
import functools
import math

import jax
import jax.numpy as jnp
from jax import lax
from jax.experimental import pallas as pl
from jax.experimental.pallas import tpu as pltpu
from jax.sharding import PartitionSpec as P

J = 16
TEAM = 4
CHUNKS = 8
HIGH = lax.Precision.HIGHEST
NT = (((1,), (1,)), ((), ()))


def split3(value):
    high = value.astype(jnp.bfloat16)
    rest = value - high.astype(jnp.float32)
    middle = rest.astype(jnp.bfloat16)
    low = (rest - middle.astype(jnp.float32)).astype(jnp.bfloat16)
    return high, middle, low


def inverse_factor(gram):
    size = gram.shape[0]
    rows = lax.broadcasted_iota(jnp.int32, (size, 128), 0)
    lanes = lax.broadcasted_iota(jnp.int32, (size, 128), 1)
    work = gram + jnp.where(lanes == rows + size, 1.0, 0.0)
    for step in range(size):
        pivot_row = work[step : step + 1, :]
        unit_row = pivot_row / pivot_row[:, step : step + 1]
        work = jnp.where(rows > step, work - work[:, step : step + 1] * unit_row, work)
    pivots = jnp.sum(jnp.where(lanes == rows, work, 0.0), axis=1, keepdims=True)
    scale = lax.rsqrt(pivots)
    work = work * (scale * (1.5 - 0.5 * pivots * scale * scale))
    return pltpu.roll(work, 128 - size, 1)[:, :size]


def kernel(count, x_ref, omega_ref, basis_ref, coupled_ref, halo, weights, sk, own, corr, gram_acc,
           pack, gbuf, msg, rbuf, kred, kfin, xs, p1s, p1r, dns, dnr, fws, fwr, srs, srr, m0s, m0r, m1s, m1r,
           m2s, m2r):
    per, inputs, width = x_ref.shape
    rank = omega_ref.shape[0]
    quarter = width // TEAM
    piece = quarter // CHUNKS
    level_lags = per * TEAM
    reach = J - 1
    lags = halo.shape[1]
    levels = count // TEAM
    total_rows = count * per * width
    me = lax.axis_index("lag")
    level, place = me // TEAM, me % TEAM
    mates = [place, place + 1 - 2 * (place % 2), (place + 2) % TEAM, TEAM - 1 - place]
    below = lax.rem(me + count - TEAM, count)

    barrier = pltpu.get_barrier_semaphore()

    @pl.loop(1, count)
    def _(step):
        pl.semaphore_signal(barrier, inc=1, device_id={"lag": lax.rem(me + step, count)},
                            device_id_type=pl.DeviceIdType.MESH)

    pl.semaphore_wait(barrier, count - 1)

    def remote(src, dst, send, recv, target):
        return pltpu.make_async_remote_copy(
            src_ref=src, dst_ref=dst, send_sem=send, recv_sem=recv,
            device_id={"lag": target}, device_id_type=pl.DeviceIdType.MESH)

    def columns(who, k):
        return pl.ds(pl.multiple_of(who * quarter + k * piece, 128), piece)

    def spread(k, s):
        mate = mates[s]
        return remote(x_ref.at[:, :, columns(mate, k)], halo.at[k, pl.ds(per * place, per)],
                      p1s.at[k, s], p1r.at[k, place], level * TEAM + mate)

    def spread_in(k, s):
        mate = mates[s]
        dst = halo.at[k, pl.ds(per * mate, per)]
        return remote(dst, dst, p1s.at[k, s], p1r.at[k, mate], level * TEAM + mate)

    def down(k, s):
        mate = mates[s]
        src = x_ref.at[:, :, columns(place, k)] if s == 0 else halo.at[k, pl.ds(per * mate, per)]
        return remote(src, halo.at[k, pl.ds(level_lags + per * mate, per)],
                      dns.at[k, s], dnr.at[k, mate], below)

    def forward(k):
        return remote(halo.at[k, pl.ds(level_lags, reach - level_lags)],
                      halo.at[k, pl.ds(2 * level_lags, reach - level_lags)],
                      fws.at[k], fwr.at[k], below)

    def give_back(k, s):
        mate = mates[s]
        return remote(sk.at[k, pl.ds(per * mate, per)], own.at[place, k],
                      srs.at[k, s], srr.at[k, place], level * TEAM + mate)

    def give_back_in(k, s):
        mate = mates[s]
        return remote(own.at[mate, k], own.at[mate, k], srs.at[k, s], srr.at[k, mate],
                      level * TEAM + mate)

    def keep(k):
        return pltpu.make_async_copy(x_ref.at[:, :, columns(place, k)],
                                     halo.at[k, pl.ds(per * place, per)], xs.at[k])

    for k in range(CHUNKS):
        for s in (2, 3, 1):
            spread(k, s).start()

        @pl.when(level > 0)
        def _():
            down(k, 0).start()

        keep(k).start()

    for k in range(CHUNKS):
        halo[k, lags - 1] = jnp.zeros((inputs, piece), jnp.bfloat16)

    @pl.when(level >= levels - 2)
    def _():
        for k in range(CHUNKS):
            halo[k, 2 * level_lags : lags - 1] = jnp.zeros(
                (lags - 1 - 2 * level_lags, inputs, piece), jnp.bfloat16)

    @pl.when(level == levels - 1)
    def _():
        for k in range(CHUNKS):
            halo[k, level_lags : 2 * level_lags] = jnp.zeros(
                (level_lags, inputs, piece), jnp.bfloat16)

    def own_down(k):
        for s in (1, 2, 3):
            spread_in(k, s).wait_recv()

            @pl.when(level > 0)
            def _():
                down(k, s).start()

    def pass_on(k):
        @pl.when(level < levels - 1)
        def _():
            for s in range(TEAM):
                down(k, s).wait_recv()

            @pl.when(level > 0)
            def _():
                forward(k).start()

    def compute(k):
        keep(k).wait()

        @pl.when(level < levels - 2)
        def _():
            forward(k).wait_recv()

        window = halo[k].reshape(lags * inputs, piece)
        sketch = jnp.dot(weights[...], window, preferred_element_type=jnp.float32)
        sk[k] = sketch.reshape(level_lags, rank, piece)
        for s in (2, 3, 1):
            give_back(k, s).start()
        own[place, k] = sk[k, pl.ds(per * place, per)]
        wide = jnp.concatenate([sketch[i * rank : (i + 1) * rank] for i in range(level_lags)], axis=1)
        local = lax.dot_general(wide, wide, NT, precision=HIGH, preferred_element_type=jnp.float32)
        gram_acc[:, :rank] = local if k == 0 else gram_acc[:, :rank] + local
        if k == CHUNKS - 1:
            share_gram()
        parts = split3(sketch)
        product = sum(
            lax.dot_general(part, window, NT, preferred_element_type=jnp.float32)
            for part in reversed(parts)
        )
        corr[...] = product if k == 0 else corr[...] + product

    def gram_to(step):
        other = lax.rem(me + step, count)
        return remote(pack, gbuf.at[me], m0s.at[step], m0r.at[me], other)

    def gram_in(step):
        other = lax.rem(me + step, count)
        return remote(pack, gbuf.at[other], m0s.at[step], m0r.at[other], other)

    def share_gram():
        packed = gram_acc[0:8, :]
        for b in range(1, rank // 8):
            packed = packed + pltpu.roll(gram_acc[8 * b : 8 * b + 8, :], b * rank, 1)
        pack[...] = packed

        @pl.loop(1, count)
        def _(step):
            gram_to(step).start()

        gbuf[me] = packed

    own_down(0)
    own_down(1)
    gram_acc[...] = jnp.zeros_like(gram_acc)
    turned = omega_ref[...].astype(jnp.float32) * 0.25
    band = jnp.concatenate(
        [turned, jnp.zeros((rank, weights.shape[1] - turned.shape[1]), jnp.float32)], axis=1)
    for i in range(level_lags):
        row = band if i == 0 else pltpu.roll(band, i * inputs, 1)
        weights[i * rank : (i + 1) * rank, :] = row.astype(jnp.bfloat16)
    pass_on(0)
    for k in range(2, CHUNKS):
        own_down(k)
        pass_on(k - 1)
        if k > 2:
            compute(k - 3)
    compute(CHUNKS - 3)
    pass_on(CHUNKS - 1)
    compute(CHUNKS - 2)
    compute(CHUNKS - 1)

    folded = corr[0:rank, : J * inputs]
    for i in range(1, level_lags):
        turned_back = pltpu.roll(corr[i * rank : (i + 1) * rank, :], lags * inputs - i * inputs, 1)
        folded = folded + turned_back[:, : J * inputs]
    tiles_across = J * inputs // 128
    tiles = (rank // 8) * tiles_across
    for d in range(count):
        if d < tiles:
            a, b = divmod(d, tiles_across)
            msg[d] = folded[8 * a : 8 * a + 8, 128 * b : 128 * b + 128]
        else:
            msg[d] = jnp.zeros((8, 128), jnp.float32)

    def partial(step):
        other = lax.rem(me + step, count)
        return remote(msg.at[other], rbuf.at[me], m1s.at[step], m1r.at[me], other)

    def partial_in(step):
        other = lax.rem(me + step, count)
        return remote(msg.at[other], rbuf.at[other], m1s.at[step], m1r.at[other], other)

    def whole(step):
        other = lax.rem(me + step, count)
        return remote(kred, kfin.at[me], m2s.at[step], m2r.at[me], other)

    def whole_in(step):
        other = lax.rem(me + step, count)
        return remote(kred, kfin.at[other], m2s.at[step], m2r.at[other], other)

    @pl.loop(1, count)
    def _(step):
        partial(step).start()

    rbuf[me] = msg[me]

    @pl.loop(1, count)
    def _(step):
        gram_in(step).wait_recv()

    @pl.loop(1, count)
    def _(step):
        partial_in(step).wait_recv()

    product = rbuf[0]
    total = gbuf[0]
    for d in range(1, count):
        product = product + rbuf[d]
        total = total + gbuf[d]
    kred[...] = product
    kfin[me] = product

    @pl.loop(1, count)
    def _(step):
        whole(step).start()

    lanes = lax.broadcasted_iota(jnp.int32, (8, 128), 1)
    blocks = []
    for b in range(rank // 8):
        block = total if b == 0 else pltpu.roll(total, 128 - b * rank, 1)
        blocks.append(jnp.where(lanes < rank, block, 0.0))
    inverse = inverse_factor(jnp.concatenate(blocks, axis=0) * (1.0 / total_rows))

    for k in range(CHUNKS):
        for s in range(1, TEAM):
            give_back_in(k, s).wait_recv()
    for q in range(TEAM):
        for k in range(CHUNKS):
            for g in range(per):
                basis_ref[g, :, q * quarter + k * piece : q * quarter + (k + 1) * piece] = jnp.dot(
                    inverse, own[q, k, g], precision=HIGH, preferred_element_type=jnp.float32)

    @pl.loop(1, count)
    def _(step):
        whole_in(step).wait_recv()

    summed = jnp.concatenate(
        [jnp.concatenate([kfin[a * tiles_across + b] for b in range(tiles_across)], axis=1)
         for a in range(rank // 8)], axis=0)
    coupled_ref[...] = jnp.dot(
        inverse, summed, precision=HIGH, preferred_element_type=jnp.float32
    ) * (1.0 / math.sqrt(total_rows))

    for k in range(CHUNKS):
        for s in range(1, TEAM):
            spread(k, s).wait_send()
            give_back(k, s).wait_send()

    @pl.when(level > 0)
    def _():
        for k in range(CHUNKS):
            for s in range(TEAM):
                down(k, s).wait_send()

    @pl.when(jnp.logical_and(level > 0, level < levels - 1))
    def _():
        for k in range(CHUNKS):
            forward(k).wait_send()

    @pl.loop(1, count)
    def _(step):
        gram_to(step).wait_send()
        partial(step).wait_send()
        whole(step).wait_send()


def per_device(count, markov, omega):
    per, inputs, width = markov.shape
    rank = omega.shape[1]
    piece = width // TEAM // CHUNKS
    level_lags = per * TEAM
    lags = level_lags + J
    dma = pltpu.SemaphoreType.DMA
    vmem = pl.BlockSpec(memory_space=pltpu.VMEM)
    return pl.pallas_call(
        functools.partial(kernel, count),
        out_shape=(
            jax.ShapeDtypeStruct((per, rank, width), jnp.float32),
            jax.ShapeDtypeStruct((rank, J * inputs), jnp.float32),
        ),
        in_specs=[pl.BlockSpec(memory_space=pltpu.HBM), vmem],
        out_specs=(vmem, vmem),
        scratch_shapes=[
            pltpu.VMEM((CHUNKS, lags, inputs, piece), jnp.bfloat16),
            pltpu.VMEM((level_lags * rank, lags * inputs), jnp.bfloat16),
            pltpu.VMEM((CHUNKS, level_lags, rank, piece), jnp.float32),
            pltpu.VMEM((TEAM, CHUNKS, per, rank, piece), jnp.float32),
            pltpu.VMEM((level_lags * rank, lags * inputs), jnp.float32),
            pltpu.VMEM((rank, 128), jnp.float32),
            pltpu.VMEM((8, 128), jnp.float32),
            pltpu.VMEM((count, 8, 128), jnp.float32),
            pltpu.VMEM((count, 8, 128), jnp.float32),
            pltpu.VMEM((count, 8, 128), jnp.float32),
            pltpu.VMEM((8, 128), jnp.float32),
            pltpu.VMEM((count, 8, 128), jnp.float32),
            dma((CHUNKS,)),
            dma((CHUNKS, TEAM)), dma((CHUNKS, TEAM)), dma((CHUNKS, TEAM)), dma((CHUNKS, TEAM)),
            dma((CHUNKS,)), dma((CHUNKS,)), dma((CHUNKS, TEAM)), dma((CHUNKS, TEAM)),
            dma((count,)), dma((count,)), dma((count,)), dma((count,)), dma((count,)), dma((count,)),
        ],
        compiler_params=pltpu.CompilerParams(
            collective_id=0, has_side_effects=True, vmem_limit_bytes=40 * 2**20
        ),
        cost_estimate=pl.CostEstimate(flops=6 * 10**9, bytes_accessed=8 * 2**20, transcendentals=0),
    )(markov, omega.T)


def solution(mesh):
    return jax.shard_map(
        functools.partial(per_device, mesh.shape["lag"]),
        mesh=mesh,
        in_specs=(P(("group", "lag"), None, None), P()),
        out_specs=(P(("group", "lag"), None, None), P("group", None)),
        check_vma=False,
    )
```
